32 devices in a mesh: grp: 2 (over y), blk: 4 (over z), seq: 2 (over x), col: 2 (over core).
Axes of the slice: x: 2, y: 2, z: 4, core: 2. Of those that a mesh axis runs over, the one named last changes fastest.
Arguments:
- activations: bfloat16 [2048, 6912], P(('grp', 'blk', 'seq'), 'col'), parts along dimension 0, may hold values from -6 to 6
- output_grads: bfloat16 [2048, 5120], P(('grp', 'blk', 'seq')), parts along dimension 0, may hold values from -6 to 6
- queries: float32 [2, 6912, 5120], P('grp', ('col', 'blk'), 'seq'), parts along dimension 0, may hold values from -6.1035156e-05 to 6.1035156e-05
- lengths: int32 [8], P(('grp', 'blk')), parts along dimension 0, may hold values from 32 to 256, as said below
- assignment: int32 [8], P('grp'), parts along dimension 0, may hold values from 0 to 3, each once
Outputs:
- scores: float32 [1, 8], P(None, ('grp', 'blk')), parts along dimension 1
The draws below stay inside these ranges and needn't reach their ends.
There are 2 independent parts, one for each index of `grp`. The reference program is written for one: setup_inputs(seed, part) draws one part's arguments, and reference() takes and returns one part's arrays. A program takes and returns all parts, laid end to end along the dimension named above; each array names one. Nothing has to cross between parts.
Inputs may be any that keep to these rules, and one draw needn't show every extreme that they name: `lengths`: one slot of each part holds a document of exactly 256 valid tokens. `assignment`: each document is held by exactly one slot.
All inputs are finite; a program needn't handle non-finite values.
Results may differ from the reference program's by a relative error of at most 0.0003.
Values may be sent and summed in bfloat16 or wider, within the bound.
A program may use at most 128 MiB of HBM per device.

```python
import jax
import jax.numpy as jnp
from jax import lax

D = 5120
FF_WIN = 6912
LSEQ = 128
NQ = 1
LEN = 256
DOCS = 4
TOKENS = 1024
N_SEQ = 2


def draw_lengths(key, part):
    key = jax.random.fold_in(key, 11)
    key_len, key_pick = jax.random.split(key)
    lengths_drawn = jax.random.randint(key_len, (DOCS,), LEN // 8, LEN + 1)
    chosen = jax.random.randint(key_pick, (), 0, DOCS)
    return jnp.where(jnp.arange(DOCS) == chosen, LEN, lengths_drawn).astype(jnp.int32)


def levels(stream_key, dims, cuts, least, high):
    def one(axis_at, blocks):
        steps = jax.random.uniform(jax.random.fold_in(jax.random.fold_in(stream_key, 6), axis_at), (blocks,), jnp.float32, least / len(cuts), high / len(cuts))
        return jnp.repeat(jnp.exp(steps), dims[axis_at] // blocks).reshape((-1,) + (1,) * (len(dims) - axis_at - 1))

    gain = one(*cuts[0])
    for cut in cuts[1:]:
        gain = gain * one(*cut)
    return gain


def scatter_about(rng, shape, width, limit, cuts=(), kind=jnp.bfloat16):
    entries = width * jax.random.normal(rng, shape, jnp.float32)
    if cuts:
        entries = entries * levels(rng, shape, cuts, -0.22, 0.18)
    return jnp.clip(entries, -limit, limit).astype(kind)


def setup_inputs(seed: int = 0, part: int = 0) -> dict:
    key_of = jax.random.split(jax.random.key(seed), 6)
    part_keys = jax.random.split(jax.random.fold_in(key_of[5], part), 6)
    activations = scatter_about(part_keys[0], (TOKENS, FF_WIN), 1.0, 6.0, ((0, 8), (1, 2)))
    output_grads = scatter_about(part_keys[1], (TOKENS, D), 1.0, 6.0, ((0, 8),))
    queries = scatter_about(part_keys[2], (NQ, FF_WIN, D), (LSEQ * N_SEQ * FF_WIN * D) ** -0.5, 6.103515625e-05, ((1, 8), (2, 2)), jnp.float32)
    lengths = draw_lengths(jax.random.fold_in(jax.random.fold_in(key_of[5], part), 71), part)
    assignment = jax.random.permutation(part_keys[4], DOCS).astype(jnp.int32)
    return {"activations": activations, "output_grads": output_grads, "queries": queries, "lengths": lengths, "assignment": assignment}


def reference(activations, output_grads, queries, lengths, assignment):
    act_docs = activations.reshape(DOCS, LEN, FF_WIN)
    grad_docs = output_grads.reshape(DOCS, LEN, D)
    positions = jnp.arange(LEN, dtype=jnp.int32)

    def one_slot(inputs):
        act_rows, grad_rows, length = inputs
        masked = jnp.where((positions < length)[:, None], grad_rows, jnp.zeros_like(grad_rows))
        grad_block = jnp.dot(act_rows.T, masked, preferred_element_type=jnp.float32)
        return jnp.einsum("qfd,fd->q", queries, grad_block, precision=lax.Precision.HIGHEST)

    slot_values = lax.map(one_slot, (act_docs, grad_docs, lengths))
    return jnp.zeros((NQ, DOCS), jnp.float32).at[:, assignment].set(slot_values.T)
```

```python
import functools

import jax
import jax.numpy as jnp
from jax import lax
from jax.experimental import pallas as pl
from jax.experimental.pallas import tpu as pltpu
from jax.sharding import PartitionSpec as P

MESH = pl.DeviceIdType.MESH


def score_kernel(
    nb, ns, nc,
    a_ref, g_ref, q_ref, assign_ref, out_ref,
    g_all, a_all, q_vmem, part, mine, others,
    local_sem, g_recv, g_right, g_left, g_side, g_x,
    a_recv, a_z, a_x, p_send, p_recv,
):
    b = lax.axis_index("blk")
    s = lax.axis_index("seq")
    c = lax.axis_index("col")
    rows = g_ref.shape[0]
    share = rows // nc
    fp, dl = q_ref.shape[1], q_ref.shape[2]
    my_rows = pl.multiple_of(c * share, share)
    n_dev = nb * ns * nc

    def device(db, ds, dc):
        return {
            "blk": lax.rem(b + db, nb),
            "seq": lax.rem(s + ds, ns),
            "col": lax.rem(c + dc, nc),
        }

    def offsets(t):
        return t // (ns * nc), lax.rem(t // nc, ns), lax.rem(t, nc)

    barrier = pltpu.get_barrier_semaphore()

    @pl.loop(1, n_dev)
    def _(t):
        pl.semaphore_signal(barrier, inc=1, device_id=device(*offsets(t)), device_id_type=MESH)

    def g_rows(tb, cc):
        return pl.ds(pl.multiple_of(tb * rows + cc * share, share), share)

    def g_copy(src, doc, tb, sem, to):
        return pltpu.make_async_remote_copy(
            src_ref=src,
            dst_ref=g_all.at[doc, g_rows(tb, c)],
            send_sem=sem,
            recv_sem=g_recv.at[doc, tb, c],
            device_id=to,
            device_id_type=MESH,
        )

    def g_landed(doc, tb, cc):
        pltpu.make_async_copy(
            g_all.at[doc, g_rows(tb, cc)], g_all.at[doc, g_rows(tb, cc)], g_recv.at[doc, tb, cc]
        ).wait()

    def own_columns(tb):
        return g_ref.at[pl.ds(my_rows, share), pl.ds(pl.multiple_of(tb * dl, 128), dl)]

    def right_copy(src, doc, tb):
        return g_copy(src, doc, tb, g_right.at[doc, tb], {"blk": b + 1})

    def left_copy(src, doc, tb):
        return g_copy(src, doc, tb, g_left.at[doc, tb], {"blk": b - 1})

    def side_copy(doc, tb):
        return g_copy(
            g_all.at[doc, g_rows(tb, c)], doc, tb, g_side.at[doc, tb], device(0, 0, 1)
        )

    def x_copy(ds):
        return g_copy(own_columns(lax.rem(s + ds, ns)), b, s, g_x.at[ds - 1], device(0, ds, 0))

    def a_z_copy(db):
        to = lax.rem(b + db, nb)
        return pltpu.make_async_remote_copy(
            src_ref=a_ref.at[to],
            dst_ref=a_all.at[b, s],
            send_sem=a_z.at[db - 1],
            recv_sem=a_recv.at[b, s],
            device_id={"blk": to},
            device_id_type=MESH,
        )

    def a_x_copy(src, doc, ds):
        return pltpu.make_async_remote_copy(
            src_ref=src,
            dst_ref=a_all.at[doc, s],
            send_sem=a_x.at[doc, ds - 1],
            recv_sem=a_recv.at[doc, s],
            device_id=device(0, ds, 0),
            device_id_type=MESH,
        )

    def a_landed(doc, tb):
        pltpu.make_async_copy(a_all.at[doc, tb], a_all.at[doc, tb], a_recv.at[doc, tb]).wait()

    q_copy = pltpu.make_async_copy(q_ref.at[0], q_vmem, local_sem.at[0])
    own_g_copy = pltpu.make_async_copy(
        g_ref.at[:, pl.ds(pl.multiple_of(s * dl, 128), dl)],
        g_all.at[b, pl.ds(pl.multiple_of(s * rows, rows), rows)],
        local_sem.at[1],
    )
    own_a_copy = pltpu.make_async_copy(a_ref.at[b], a_all.at[b, s], local_sem.at[2])
    own_g_copy.start()
    own_a_copy.start()
    q_copy.start()

    pl.semaphore_wait(barrier, n_dev - 1)

    for ds in range(1, ns):
        x_copy(ds).start()

    @pl.when(b < nb - 1)
    def _():
        right_copy(own_columns(s), b, s).start()

    @pl.when(b > 0)
    def _():
        left_copy(own_columns(s), b, s).start()

    for db in range(1, nb):
        a_z_copy(db).start()
    for ds in range(1, ns):
        a_x_copy(a_ref.at[b], b, ds).start()

    def score(doc):
        for ds in range(1, ns):
            a_landed(doc, lax.rem(s + ds, ns))
        lhs = jnp.concatenate([a_all[doc, tb] for tb in range(ns)], axis=1)
        tile = 256 if dl % 256 == 0 else 128

        def one_tile(i, acc):
            columns = pl.ds(pl.multiple_of(i * tile, tile), tile)
            grad = jnp.dot(lhs, g_all[doc, :, columns], preferred_element_type=jnp.float32)
            prod = grad * q_vmem[:, columns]
            return acc + jnp.sum(prod.reshape(fp // 8, 8, tile), axis=0)

        acc = lax.fori_loop(0, dl // tile, one_tile, jnp.zeros((8, tile), jnp.float32))
        part[doc] = sum(acc[:, i * 128:(i + 1) * 128] for i in range(tile // 128))

    for ds in range(1, ns):
        tb = lax.rem(s + ds, ns)
        g_landed(b, tb, c)
        src = g_all.at[b, g_rows(tb, c)]

        @pl.when(b < nb - 1)
        def _():
            right_copy(src, b, tb).start()

        @pl.when(b > 0)
        def _():
            left_copy(src, b, tb).start()

        side_copy(b, tb).start()

    def relay(doc, onward, may_go_on):
        a_landed(doc, s)
        for ds in range(1, ns):
            a_x_copy(a_all.at[doc, s], doc, ds).start()
        for ds in range(ns):
            tb = lax.rem(s + ds, ns)
            g_landed(doc, tb, c)

            @pl.when(may_go_on)
            def _():
                onward(g_all.at[doc, g_rows(tb, c)], doc, tb).start()

            side_copy(doc, tb).start()

    def score_far(doc):
        for tb in range(ns):
            g_landed(doc, tb, 1 - c)
        score(doc)

    def from_left(k, act):
        @pl.when(b - k >= 0)
        def _():
            act(b - k)

    def from_right(k, act):
        @pl.when(b + k < nb)
        def _():
            act(b + k)

    def score_own():
        own_a_copy.wait()
        own_g_copy.wait()
        q_copy.wait()
        for ds in range(1, ns):
            g_landed(b, lax.rem(s + ds, ns), 1 - c)
        score(b)

    for k in range(1, nb):
        from_left(k, lambda doc: relay(doc, right_copy, b < nb - 1))
        from_right(k, lambda doc: relay(doc, left_copy, b > 0))
        if k == 1:
            score_own()
        else:
            from_left(k - 1, score_far)
            from_right(k - 1, score_far)
    from_left(nb - 1, score_far)
    from_right(nb - 1, score_far)

    mine[...] = jnp.concatenate([jnp.sum(part[j], axis=0, keepdims=True) for j in range(nb)], axis=0)

    def p_copy(t):
        return pltpu.make_async_remote_copy(
            src_ref=mine,
            dst_ref=others.at[t],
            send_sem=p_send.at[t],
            recv_sem=p_recv.at[t],
            device_id=device(*offsets(t)),
            device_id_type=MESH,
        )

    @pl.loop(1, n_dev)
    def _(t):
        p_copy(t).start()

    for ds in range(1, ns):
        x_copy(ds).wait_send()
        a_x_copy(a_ref.at[b], b, ds).wait_send()
    for db in range(1, nb):
        a_z_copy(db).wait_send()

    @pl.when(b < nb - 1)
    def _():
        right_copy(own_columns(s), b, s).wait_send()

    @pl.when(b > 0)
    def _():
        left_copy(own_columns(s), b, s).wait_send()

    for ds in range(1, ns):
        tb = lax.rem(s + ds, ns)
        src = g_all.at[b, g_rows(tb, c)]

        @pl.when(b < nb - 1)
        def _():
            right_copy(src, b, tb).wait_send()

        @pl.when(b > 0)
        def _():
            left_copy(src, b, tb).wait_send()

        side_copy(b, tb).wait_send()

    def relay_sent(doc, onward, may_go_on):
        for ds in range(1, ns):
            a_x_copy(a_all.at[doc, s], doc, ds).wait_send()
        for ds in range(ns):
            tb = lax.rem(s + ds, ns)

            @pl.when(may_go_on)
            def _():
                onward(g_all.at[doc, g_rows(tb, c)], doc, tb).wait_send()

            side_copy(doc, tb).wait_send()

    for k in range(1, nb):
        from_left(k, lambda doc: relay_sent(doc, right_copy, b < nb - 1))
        from_right(k, lambda doc: relay_sent(doc, left_copy, b > 0))

    @pl.loop(1, n_dev)
    def _(t):
        p_copy(t).wait()

    def add_one(t, total):
        return total + others[t]

    total = lax.fori_loop(1, n_dev, add_one, mine[...])
    chosen = jnp.zeros((1, 128), jnp.float32)
    for j in range(nb):
        chosen = chosen + jnp.where(assign_ref[j] == b, total[j:j + 1], 0.0)
    out_ref[...] = jnp.sum(chosen, axis=1, keepdims=True)


def on_device(activations, output_grads, queries, lengths, assignment):
    nb, ns, nc = lax.axis_size("blk"), lax.axis_size("seq"), lax.axis_size("col")
    rows, d_model = output_grads.shape
    fp, dl = queries.shape[1], queries.shape[2]
    positions = lax.axis_index("seq") * rows + jnp.arange(rows, dtype=jnp.int32)
    masked = jnp.where((positions < lengths[0])[:, None], activations, jnp.zeros_like(activations))
    panels = masked.reshape(rows, nb, fp).transpose(1, 2, 0)
    n_dev = nb * ns * nc
    dma = pltpu.SemaphoreType.DMA
    return pl.pallas_call(
        functools.partial(score_kernel, nb, ns, nc),
        out_shape=jax.ShapeDtypeStruct((1, 1), jnp.float32),
        in_specs=[
            pl.BlockSpec(memory_space=pl.ANY),
            pl.BlockSpec(memory_space=pl.ANY),
            pl.BlockSpec(memory_space=pl.ANY),
            pl.BlockSpec(memory_space=pltpu.SMEM),
        ],
        out_specs=pl.BlockSpec(memory_space=pltpu.VMEM),
        scratch_shapes=[
            pltpu.VMEM((nb, ns * rows, dl), jnp.bfloat16),
            pltpu.VMEM((nb, ns, fp, rows), jnp.bfloat16),
            pltpu.VMEM((fp, dl), jnp.float32),
            pltpu.VMEM((nb, 8, 128), jnp.float32),
            pltpu.VMEM((nb, 128), jnp.float32),
            pltpu.VMEM((n_dev, nb, 128), jnp.float32),
            dma((3,)),
            dma((nb, ns, nc)),
            dma((nb, ns)),
            dma((nb, ns)),
            dma((nb, ns)),
            dma((max(ns - 1, 1),)),
            dma((nb, ns)),
            dma((max(nb - 1, 1),)),
            dma((nb, max(ns - 1, 1))),
            dma((n_dev,)),
            dma((n_dev,)),
        ],
        compiler_params=pltpu.CompilerParams(
            collective_id=0, has_side_effects=True, vmem_limit_bytes=56 * 1024 * 1024
        ),
        cost_estimate=pl.CostEstimate(
            flops=2 * nb * ns * rows * fp * dl, bytes_accessed=4 * fp * dl, transcendentals=0
        ),
    )(panels, output_grads, queries, assignment)


def solution(mesh):
    in_specs = (
        P(("grp", "blk", "seq"), "col"),
        P(("grp", "blk", "seq"), None),
        P("grp", ("col", "blk"), "seq"),
        P(("grp", "blk")),
        P("grp"),
    )
    out_specs = P(None, ("grp", "blk"))
    return jax.shard_map(
        on_device, mesh=mesh, in_specs=in_specs, out_specs=out_specs, check_vma=False
    )
```

```python
import functools

import jax
import jax.numpy as jnp
from jax import lax
from jax.experimental import pallas as pl
from jax.experimental.pallas import tpu as pltpu
from jax.sharding import PartitionSpec as P

MESH = pl.DeviceIdType.MESH


def score_kernel(
    nb, ns, nc,
    a_ref, g_ref, q_ref, length_ref, assign_ref, out_ref,
    g_all, a_all, a_own, a_panels, q_vmem, q_high, q_low, a_doc, y_doc,
    y_out, y_in, y_sum, y_far, part, mine, others,
    local_sem, g_recv, g_right, g_left, g_side, g_x,
    a_recv, a_z, a_x, y_send, y_recv, p_send, p_recv,
):
    b = lax.axis_index("blk")
    s = lax.axis_index("seq")
    c = lax.axis_index("col")
    rows = g_ref.shape[0]
    share = rows // nc
    fp, dl = q_vmem.shape
    tile = next(t for t in (512, 256, 128) if dl % t == 0)
    my_rows = pl.multiple_of(c * share, share)
    n_dev = nb * ns * nc

    def device(db, ds, dc):
        return {
            "blk": lax.rem(b + db, nb),
            "seq": lax.rem(s + ds, ns),
            "col": lax.rem(c + dc, nc),
        }

    def offsets(t):
        return t // (ns * nc), lax.rem(t // nc, ns), lax.rem(t, nc)

    barrier = pltpu.get_barrier_semaphore()

    @pl.loop(1, n_dev)
    def _(t):
        pl.semaphore_signal(barrier, inc=1, device_id=device(*offsets(t)), device_id_type=MESH)

    a_copy = pltpu.make_async_copy(a_ref, a_own, local_sem.at[2])
    q_copy = pltpu.make_async_copy(q_ref.at[0], q_vmem, local_sem.at[0])
    own_g_copy = pltpu.make_async_copy(
        g_ref.at[:, pl.ds(pl.multiple_of(s * dl, 128), dl)],
        g_all.at[b, pl.ds(pl.multiple_of(s * rows, rows), rows)],
        local_sem.at[1],
    )
    a_copy.start()
    own_g_copy.start()
    q_copy.start()

    def g_rows(tb, cc):
        return pl.ds(pl.multiple_of(tb * rows + cc * share, share), share)

    def g_copy(src, doc, tb, sem, to):
        return pltpu.make_async_remote_copy(
            src_ref=src,
            dst_ref=g_all.at[doc, g_rows(tb, c)],
            send_sem=sem,
            recv_sem=g_recv.at[doc, tb, c],
            device_id=to,
            device_id_type=MESH,
        )

    def g_landed(doc, tb, cc):
        pltpu.make_async_copy(
            g_all.at[doc, g_rows(tb, cc)], g_all.at[doc, g_rows(tb, cc)], g_recv.at[doc, tb, cc]
        ).wait()

    def own_columns(tb):
        return g_ref.at[pl.ds(my_rows, share), pl.ds(pl.multiple_of(tb * dl, 128), dl)]

    def right_copy(src, doc, tb):
        return g_copy(src, doc, tb, g_right.at[doc, tb], {"blk": b + 1})

    def left_copy(src, doc, tb):
        return g_copy(src, doc, tb, g_left.at[doc, tb], {"blk": b - 1})

    def side_copy(doc, tb):
        return g_copy(
            g_all.at[doc, g_rows(tb, c)], doc, tb, g_side.at[doc, tb], device(0, 0, 1)
        )

    def x_copy(ds):
        return g_copy(own_columns(lax.rem(s + ds, ns)), b, s, g_x.at[ds - 1], device(0, ds, 0))

    def a_z_copy(db):
        to = lax.rem(b + db, nb)
        return pltpu.make_async_remote_copy(
            src_ref=a_panels.at[to],
            dst_ref=a_all.at[b, s],
            send_sem=a_z.at[db - 1],
            recv_sem=a_recv.at[b, s],
            device_id={"blk": to},
            device_id_type=MESH,
        )

    def a_x_copy(src, doc, ds):
        return pltpu.make_async_remote_copy(
            src_ref=src,
            dst_ref=a_all.at[doc, s],
            send_sem=a_x.at[doc, ds - 1],
            recv_sem=a_recv.at[doc, s],
            device_id=device(0, ds, 0),
            device_id_type=MESH,
        )

    def a_landed(doc, tb):
        pltpu.make_async_copy(a_all.at[doc, tb], a_all.at[doc, tb], a_recv.at[doc, tb]).wait()

    y_side_copy = pltpu.make_async_remote_copy(
        src_ref=y_out.at[pl.ds(pl.multiple_of((1 - c) * share, share), share)],
        dst_ref=y_in,
        send_sem=y_send.at[0],
        recv_sem=y_recv.at[2],
        device_id=device(0, 0, 1),
        device_id_type=MESH,
    )

    def y_z_copy(side, to):
        return pltpu.make_async_remote_copy(
            src_ref=y_sum,
            dst_ref=y_far.at[side],
            send_sem=y_send.at[1],
            recv_sem=y_recv.at[side],
            device_id={"blk": to},
            device_id_type=MESH,
        )

    positions = s * rows + lax.broadcasted_iota(jnp.int32, (rows, 1), 0)
    valid = jnp.where(positions < length_ref[0], 1.0, 0.0).astype(jnp.bfloat16)
    a_copy.wait()
    for p in range(nb):
        a_panels[p] = (a_own[:, p * fp:(p + 1) * fp] * valid).T

    pl.semaphore_wait(barrier, n_dev - 1)

    for db in range(1, nb):
        a_z_copy(db).start()
    for ds in range(1, ns):
        x_copy(ds).start()

    @pl.when(b < nb - 2)
    def _():
        right_copy(own_columns(s), b, s).start()

    @pl.when(b > 1)
    def _():
        left_copy(own_columns(s), b, s).start()

    for ds in range(1, ns):
        a_x_copy(a_panels.at[b], b, ds).start()

    part[...] = jnp.zeros_like(part)
    q_copy.wait()
    step_rows = next(t for t in (96, 72, 8) if fp % t == 0)

    @pl.loop(0, fp // step_rows)
    def _(i):
        here = pl.ds(pl.multiple_of(i * step_rows, step_rows), step_rows)
        value = q_vmem[here, :]
        high = value.astype(jnp.bfloat16)
        q_high[here, :] = high
        q_low[here, :] = (value - high.astype(jnp.float32)).astype(jnp.bfloat16)

    def a_relay(doc):
        a_landed(doc, s)
        for ds in range(1, ns):
            a_x_copy(a_all.at[doc, s], doc, ds).start()

    def products(a_rows, store):
        @pl.loop(0, dl // tile)
        def _(i):
            columns = pl.ds(pl.multiple_of(i * tile, tile), tile)
            store(
                columns,
                jnp.dot(a_rows[...], q_high[:, columns], preferred_element_type=jnp.float32)
                + jnp.dot(a_rows[...], q_low[:, columns], preferred_element_type=jnp.float32),
            )

    def doc_products(doc, slot, own):
        for tb in range(ns):
            def take(ref):
                a_doc[tb * rows:(tb + 1) * rows, :] = ref[...].T

            if own:
                @pl.when(tb == s)
                def _():
                    take(a_panels.at[doc])

                @pl.when(tb != s)
                def _():
                    a_landed(doc, tb)
                    take(a_all.at[doc, tb])
            else:
                @pl.when(tb != s)
                def _():
                    a_landed(doc, tb)

                take(a_all.at[doc, tb])

        def store(columns, value):
            y_doc[slot, :, columns] = value

        products(a_doc, store)

    def add_product(doc, y, g):
        count = y.shape[0]

        def one_tile(i, acc):
            columns = pl.ds(pl.multiple_of(i * tile, tile), tile)
            prod = y[:, columns] * g[:, columns].astype(jnp.float32)
            return acc + jnp.sum(prod.reshape(count // 8, 8, tile), axis=0)

        acc = lax.fori_loop(0, dl // tile, one_tile, jnp.zeros((8, tile), jnp.float32))
        part[doc] += sum(acc[:, i * 128:(i + 1) * 128] for i in range(tile // 128))

    def add_block(doc, slot, tb):
        here = pl.ds(pl.multiple_of(tb * rows, rows), rows)
        add_product(doc, y_doc.at[slot, here], g_all.at[doc, here])

    def from_left(k, act):
        @pl.when(b - k >= 0)
        def _():
            act(b - k)

    def from_right(k, act):
        @pl.when(b + k < nb)
        def _():
            act(b + k)

    at_right_end = b == nb - 1
    at_left_end = b == 0

    from_left(1, a_relay)
    from_right(1, a_relay)

    def give_products(doc, side):
        a_doc[0:rows, :] = a_all[doc, s].T

        def store(columns, value):
            y_out[:, columns] = value

        products(a_doc.at[0:rows], store)
        y_side_copy.start()
        y_side_copy.wait_recv()
        y_sum[...] = y_out[pl.ds(my_rows, share), :] + y_in[...]
        y_z_copy(side, doc).start()

    @pl.when(at_left_end)
    def _():
        give_products(b + 1, 0)

    @pl.when(at_right_end)
    def _():
        give_products(b - 1, 1)

    for ds in range(1, ns):
        tb = lax.rem(s + ds, ns)
        g_landed(b, tb, c)
        src = g_all.at[b, g_rows(tb, c)]

        @pl.when(b < nb - 1)
        def _():
            right_copy(src, b, tb).start()

        @pl.when(b > 0)
        def _():
            left_copy(src, b, tb).start()

        side_copy(b, tb).start()

    def relay(doc, tb, onward, may_go_on):
        g_landed(doc, tb, c)

        @pl.when(may_go_on)
        def _():
            onward(g_all.at[doc, g_rows(tb, c)], doc, tb).start()

        side_copy(doc, tb).start()

    def add_far(doc, slot, tb):
        g_landed(doc, tb, 1 - c)
        add_block(doc, slot, tb)

    def sides(k, ds):
        left, right = b - k >= 0, b + k < nb
        if k == 1 and ds == 0:
            left, right = left & (b < nb - 1), right & (b > 0)
        return left, right

    doc_products(b, 0, True)
    own_g_copy.wait()
    add_block(b, 0, s)
    for ds in range(1, ns):
        tb = lax.rem(s + ds, ns)
        g_landed(b, tb, 1 - c)
        add_block(b, 0, tb)

    for k in range(1, nb):
        if k + 1 < nb:
            from_left(k + 1, a_relay)
            from_right(k + 1, a_relay)
        from_left(k, lambda doc: doc_products(doc, 0, False))
        from_right(k, lambda doc: doc_products(doc, 1, False))
        for ds in range(ns):
            tb = lax.rem(s + ds, ns)
            left, right = sides(k, ds)

            @pl.when(left)
            def _():
                relay(b - k, tb, right_copy, b < nb - 1)

            @pl.when(right)
            def _():
                relay(b + k, tb, left_copy, b > 0)

            @pl.when(left)
            def _():
                add_far(b - k, 0, tb)

            @pl.when(right)
            def _():
                add_far(b + k, 1, tb)

        if k == 1:
            own_here = g_all.at[b, g_rows(s, c)]

            def take_products(side):
                y_z_copy(side, b).wait_recv()
                add_product(b, y_far.at[side], own_here)

            @pl.when(b == 1)
            def _():
                take_products(0)

            @pl.when(b == nb - 2)
            def _():
                take_products(1)

    mine[...] = jnp.concatenate([jnp.sum(part[j], axis=0, keepdims=True) for j in range(nb)], axis=0)

    def p_copy(t):
        return pltpu.make_async_remote_copy(
            src_ref=mine,
            dst_ref=others.at[t],
            send_sem=p_send.at[t],
            recv_sem=p_recv.at[t],
            device_id=device(*offsets(t)),
            device_id_type=MESH,
        )

    @pl.loop(1, n_dev)
    def _(t):
        p_copy(t).start()

    for ds in range(1, ns):
        x_copy(ds).wait_send()
        a_x_copy(a_panels.at[b], b, ds).wait_send()
    for db in range(1, nb):
        a_z_copy(db).wait_send()

    @pl.when(at_left_end)
    def _():
        y_side_copy.wait_send()
        y_z_copy(0, b + 1).wait_send()

    @pl.when(at_right_end)
    def _():
        y_side_copy.wait_send()
        y_z_copy(1, b - 1).wait_send()

    @pl.when(b < nb - 2)
    def _():
        right_copy(own_columns(s), b, s).wait_send()

    @pl.when(b > 1)
    def _():
        left_copy(own_columns(s), b, s).wait_send()

    for ds in range(1, ns):
        tb = lax.rem(s + ds, ns)
        src = g_all.at[b, g_rows(tb, c)]

        @pl.when(b < nb - 1)
        def _():
            right_copy(src, b, tb).wait_send()

        @pl.when(b > 0)
        def _():
            left_copy(src, b, tb).wait_send()

        side_copy(b, tb).wait_send()

    def a_relay_sent(doc):
        for ds in range(1, ns):
            a_x_copy(a_all.at[doc, s], doc, ds).wait_send()

    def relay_sent(doc, tb, onward, may_go_on):
        @pl.when(may_go_on)
        def _():
            onward(g_all.at[doc, g_rows(tb, c)], doc, tb).wait_send()

        side_copy(doc, tb).wait_send()

    for k in range(1, nb):
        from_left(k, a_relay_sent)
        from_right(k, a_relay_sent)
        for ds in range(ns):
            tb = lax.rem(s + ds, ns)
            left, right = sides(k, ds)

            @pl.when(left)
            def _():
                relay_sent(b - k, tb, right_copy, b < nb - 1)

            @pl.when(right)
            def _():
                relay_sent(b + k, tb, left_copy, b > 0)

    @pl.loop(1, n_dev)
    def _(t):
        p_copy(t).wait()

    def add_one(t, total):
        return total + others[t]

    total = lax.fori_loop(1, n_dev, add_one, mine[...])
    chosen = jnp.zeros((1, 128), jnp.float32)
    for j in range(nb):
        chosen = chosen + jnp.where(assign_ref[j] == b, total[j:j + 1], 0.0)
    out_ref[...] = jnp.sum(chosen, axis=1, keepdims=True)


def on_device(activations, output_grads, queries, lengths, assignment):
    nb, ns, nc = lax.axis_size("blk"), lax.axis_size("seq"), lax.axis_size("col")
    rows = output_grads.shape[0]
    fp, dl = queries.shape[1], queries.shape[2]
    n_dev = nb * ns * nc
    dma = pltpu.SemaphoreType.DMA
    return pl.pallas_call(
        functools.partial(score_kernel, nb, ns, nc),
        out_shape=jax.ShapeDtypeStruct((1, 1), jnp.float32),
        in_specs=[
            pl.BlockSpec(memory_space=pl.ANY),
            pl.BlockSpec(memory_space=pl.ANY),
            pl.BlockSpec(memory_space=pl.ANY),
            pl.BlockSpec(memory_space=pltpu.SMEM),
            pl.BlockSpec(memory_space=pltpu.SMEM),
        ],
        out_specs=pl.BlockSpec(memory_space=pltpu.VMEM),
        scratch_shapes=[
            pltpu.VMEM((nb, ns * rows, dl), jnp.bfloat16),
            pltpu.VMEM((nb, ns, fp, rows), jnp.bfloat16),
            pltpu.VMEM((rows, nb * fp), jnp.bfloat16),
            pltpu.VMEM((nb, fp, rows), jnp.bfloat16),
            pltpu.VMEM((fp, dl), jnp.float32),
            pltpu.VMEM((fp, dl), jnp.bfloat16),
            pltpu.VMEM((fp, dl), jnp.bfloat16),
            pltpu.VMEM((ns * rows, fp), jnp.bfloat16),
            pltpu.VMEM((2, ns * rows, dl), jnp.float32),
            pltpu.VMEM((rows, dl), jnp.float32),
            pltpu.VMEM((rows // nc, dl), jnp.float32),
            pltpu.VMEM((rows // nc, dl), jnp.float32),
            pltpu.VMEM((2, rows // nc, dl), jnp.float32),
            pltpu.VMEM((nb, 8, 128), jnp.float32),
            pltpu.VMEM((nb, 128), jnp.float32),
            pltpu.VMEM((n_dev, nb, 128), jnp.float32),
            dma((3,)),
            dma((nb, ns, nc)),
            dma((nb, ns)),
            dma((nb, ns)),
            dma((nb, ns)),
            dma((max(ns - 1, 1),)),
            dma((nb, ns)),
            dma((max(nb - 1, 1),)),
            dma((nb, max(ns - 1, 1))),
            dma((2,)),
            dma((3,)),
            dma((n_dev,)),
            dma((n_dev,)),
        ],
        compiler_params=pltpu.CompilerParams(
            collective_id=0, has_side_effects=True, vmem_limit_bytes=56 * 1024 * 1024
        ),
        cost_estimate=pl.CostEstimate(
            flops=2 * nb * ns * rows * fp * dl, bytes_accessed=4 * fp * dl, transcendentals=0
        ),
    )(activations, output_grads, queries, lengths, assignment)


def solution(mesh):
    in_specs = (
        P(("grp", "blk", "seq"), "col"),
        P(("grp", "blk", "seq"), None),
        P("grp", ("col", "blk"), "seq"),
        P(("grp", "blk")),
        P("grp"),
    )
    out_specs = P(None, ("grp", "blk"))
    return jax.shard_map(
        on_device, mesh=mesh, in_specs=in_specs, out_specs=out_specs, check_vma=False
    )
```

```python
import functools

import jax
import jax.numpy as jnp
from jax import lax
from jax.experimental import pallas as pl
from jax.experimental.pallas import tpu as pltpu
from jax.sharding import PartitionSpec as P

MESH = pl.DeviceIdType.MESH


def score_kernel(
    nb, ns, nc,
    a_ref, g_ref, q_ref, length_ref, assign_ref, out_ref,
    g_all, a_all, a_own, a_panels, q_vmem, q_high, q_low, a_doc, y_doc,
    y_out, y_in, y_sum, y_far, part, mine, others,
    local_sem, g_recv, g_right, g_left, g_side, g_x,
    a_recv, a_z, a_x, y_send, y_recv, p_send, p_recv,
):
    b = lax.axis_index("blk")
    s = lax.axis_index("seq")
    c = lax.axis_index("col")
    rows = g_ref.shape[0]
    share = rows // nc
    fp, dl = q_vmem.shape
    tile = next(t for t in (512, 256, 128) if dl % t == 0)
    my_rows = pl.multiple_of(c * share, share)
    n_dev = nb * ns * nc

    def device(db, ds, dc):
        return {
            "blk": lax.rem(b + db, nb),
            "seq": lax.rem(s + ds, ns),
            "col": lax.rem(c + dc, nc),
        }

    def offsets(t):
        return t // (ns * nc), lax.rem(t // nc, ns), lax.rem(t, nc)

    barrier = pltpu.get_barrier_semaphore()

    @pl.loop(1, n_dev)
    def _(t):
        pl.semaphore_signal(barrier, inc=1, device_id=device(*offsets(t)), device_id_type=MESH)

    a_copy = pltpu.make_async_copy(a_ref, a_own, local_sem.at[2])
    q_copy = pltpu.make_async_copy(q_ref.at[0], q_vmem, local_sem.at[0])
    own_g_copy = pltpu.make_async_copy(
        g_ref.at[:, pl.ds(pl.multiple_of(s * dl, 128), dl)],
        g_all.at[b, pl.ds(pl.multiple_of(s * rows, rows), rows)],
        local_sem.at[1],
    )
    a_copy.start()
    own_g_copy.start()
    q_copy.start()

    def g_rows(tb, cc):
        return pl.ds(pl.multiple_of(tb * rows + cc * share, share), share)

    def g_copy(src, doc, tb, sem, to):
        return pltpu.make_async_remote_copy(
            src_ref=src,
            dst_ref=g_all.at[doc, g_rows(tb, c)],
            send_sem=sem,
            recv_sem=g_recv.at[doc, tb, c],
            device_id=to,
            device_id_type=MESH,
        )

    def g_landed(doc, tb, cc):
        pltpu.make_async_copy(
            g_all.at[doc, g_rows(tb, cc)], g_all.at[doc, g_rows(tb, cc)], g_recv.at[doc, tb, cc]
        ).wait()

    def own_columns(tb):
        return g_ref.at[pl.ds(my_rows, share), pl.ds(pl.multiple_of(tb * dl, 128), dl)]

    def right_copy(src, doc, tb):
        return g_copy(src, doc, tb, g_right.at[doc, tb], {"blk": b + 1})

    def left_copy(src, doc, tb):
        return g_copy(src, doc, tb, g_left.at[doc, tb], {"blk": b - 1})

    def side_copy(doc, tb):
        return g_copy(
            g_all.at[doc, g_rows(tb, c)], doc, tb, g_side.at[doc, tb], device(0, 0, 1)
        )

    def x_copy(ds):
        return g_copy(own_columns(lax.rem(s + ds, ns)), b, s, g_x.at[ds - 1], device(0, ds, 0))

    def a_z_copy(db):
        to = lax.rem(b + db, nb)
        return pltpu.make_async_remote_copy(
            src_ref=a_panels.at[to],
            dst_ref=a_all.at[b, s],
            send_sem=a_z.at[db - 1],
            recv_sem=a_recv.at[b, s],
            device_id={"blk": to},
            device_id_type=MESH,
        )

    def a_x_copy(src, doc, ds):
        return pltpu.make_async_remote_copy(
            src_ref=src,
            dst_ref=a_all.at[doc, s],
            send_sem=a_x.at[doc, ds - 1],
            recv_sem=a_recv.at[doc, s],
            device_id=device(0, ds, 0),
            device_id_type=MESH,
        )

    def a_landed(doc, tb):
        pltpu.make_async_copy(a_all.at[doc, tb], a_all.at[doc, tb], a_recv.at[doc, tb]).wait()

    y_side_copy = pltpu.make_async_remote_copy(
        src_ref=y_out.at[pl.ds(pl.multiple_of((1 - c) * share, share), share)],
        dst_ref=y_in,
        send_sem=y_send.at[0],
        recv_sem=y_recv.at[2],
        device_id=device(0, 0, 1),
        device_id_type=MESH,
    )

    def y_z_copy(side, to):
        return pltpu.make_async_remote_copy(
            src_ref=y_sum,
            dst_ref=y_far.at[side],
            send_sem=y_send.at[1],
            recv_sem=y_recv.at[side],
            device_id={"blk": to},
            device_id_type=MESH,
        )

    positions = s * rows + lax.broadcasted_iota(jnp.int32, (rows, 1), 0)
    valid = jnp.where(positions < length_ref[0], 1.0, 0.0).astype(jnp.bfloat16)
    a_copy.wait()
    for p in range(nb):
        a_panels[p] = (a_own[:, p * fp:(p + 1) * fp] * valid).T

    pl.semaphore_wait(barrier, n_dev - 1)

    for db in range(1, nb):
        a_z_copy(db).start()
    for ds in range(1, ns):
        x_copy(ds).start()

    @pl.when(b < nb - 2)
    def _():
        right_copy(own_columns(s), b, s).start()

    @pl.when(b > 1)
    def _():
        left_copy(own_columns(s), b, s).start()

    for ds in range(1, ns):
        a_x_copy(a_panels.at[b], b, ds).start()

    part[...] = jnp.zeros_like(part)
    q_copy.wait()
    step_rows = next(t for t in (96, 72, 8) if fp % t == 0)

    @pl.loop(0, fp // step_rows)
    def _(i):
        here = pl.ds(pl.multiple_of(i * step_rows, step_rows), step_rows)
        value = q_vmem[here, :]
        high = value.astype(jnp.bfloat16)
        q_high[here, :] = high
        q_low[here, :] = (value - high.astype(jnp.float32)).astype(jnp.bfloat16)

    def a_relay(doc):
        a_landed(doc, s)
        for ds in range(1, ns):
            a_x_copy(a_all.at[doc, s], doc, ds).start()

    def products(a_rows, store):
        @pl.loop(0, dl // tile)
        def _(i):
            columns = pl.ds(pl.multiple_of(i * tile, tile), tile)
            store(
                columns,
                jnp.dot(a_rows[...], q_high[:, columns], preferred_element_type=jnp.float32)
                + jnp.dot(a_rows[...], q_low[:, columns], preferred_element_type=jnp.float32),
            )

    def doc_products(doc, slot, own):
        for tb in range(ns):
            def take(ref):
                a_doc[tb * rows:(tb + 1) * rows, :] = ref[...].T

            if own:
                @pl.when(tb == s)
                def _():
                    take(a_panels.at[doc])

                @pl.when(tb != s)
                def _():
                    a_landed(doc, tb)
                    take(a_all.at[doc, tb])
            else:
                @pl.when(tb != s)
                def _():
                    a_landed(doc, tb)

                take(a_all.at[doc, tb])

        def store(columns, value):
            y_doc[slot, :, columns] = value

        products(a_doc, store)

    def add_product(doc, y, g):
        count = y.shape[0]

        def one_tile(i, acc):
            columns = pl.ds(pl.multiple_of(i * tile, tile), tile)
            prod = y[:, columns] * g[:, columns].astype(jnp.float32)
            return acc + jnp.sum(prod.reshape(count // 8, 8, tile), axis=0)

        acc = lax.fori_loop(0, dl // tile, one_tile, jnp.zeros((8, tile), jnp.float32))
        part[doc] += sum(acc[:, i * 128:(i + 1) * 128] for i in range(tile // 128))

    def add_block(doc, slot, tb):
        here = pl.ds(pl.multiple_of(tb * rows, rows), rows)
        add_product(doc, y_doc.at[slot, here], g_all.at[doc, here])

    def from_left(k, act):
        @pl.when(b - k >= 0)
        def _():
            act(b - k)

    def from_right(k, act):
        @pl.when(b + k < nb)
        def _():
            act(b + k)

    at_right_end = b == nb - 1
    at_left_end = b == 0

    def give_products(doc, side):
        a_doc[0:rows, :] = a_all[doc, s].T

        def store(columns, value):
            y_out[:, columns] = value

        products(a_doc.at[0:rows], store)
        y_side_copy.start()
        y_side_copy.wait_recv()
        y_sum[...] = y_out[pl.ds(my_rows, share), :] + y_in[...]

    for ds in range(1, ns):
        tb = lax.rem(s + ds, ns)
        g_landed(b, tb, c)
        src = g_all.at[b, g_rows(tb, c)]

        @pl.when(b < nb - 1)
        def _():
            right_copy(src, b, tb).start()

        @pl.when(b > 0)
        def _():
            left_copy(src, b, tb).start()

        side_copy(b, tb).start()

    def a_relays(k):
        if k < nb:
            from_left(k, a_relay)
            from_right(k, a_relay)

    def relay(doc, tb, onward, may_go_on):
        g_landed(doc, tb, c)

        @pl.when(may_go_on)
        def _():
            onward(g_all.at[doc, g_rows(tb, c)], doc, tb).start()

        side_copy(doc, tb).start()

    def add_far(doc, slot, tb):
        g_landed(doc, tb, 1 - c)
        add_block(doc, slot, tb)

    def sides(k, ds):
        left, right = b - k >= 0, b + k < nb
        if k == 1 and ds == 0:
            left, right = left & (b < nb - 1), right & (b > 0)
        return left, right

    def relays(k, ds):
        tb = lax.rem(s + ds, ns)
        left, right = sides(k, ds)

        @pl.when(left)
        def _():
            relay(b - k, tb, right_copy, b < nb - 1)

        @pl.when(right)
        def _():
            relay(b + k, tb, left_copy, b > 0)

    def add_blocks(k, ds):
        tb = lax.rem(s + ds, ns)
        left, right = sides(k, ds)

        @pl.when(left)
        def _():
            add_far(b - k, 0, tb)

        @pl.when(right)
        def _():
            add_far(b + k, 1, tb)

    a_relays(1)

    @pl.when(at_left_end)
    def _():
        give_products(b + 1, 0)

    @pl.when(at_right_end)
    def _():
        give_products(b - 1, 1)

    relays(1, 0)
    a_relays(2)

    @pl.when(at_left_end)
    def _():
        for ds in range(1, ns):
            tb = lax.rem(s + ds, ns)
            right_copy(g_all.at[b, g_rows(tb, c)], b, tb).wait_send()
        y_z_copy(0, b + 1).start()

    @pl.when(at_right_end)
    def _():
        for ds in range(1, ns):
            tb = lax.rem(s + ds, ns)
            left_copy(g_all.at[b, g_rows(tb, c)], b, tb).wait_send()
        y_z_copy(1, b - 1).start()

    doc_products(b, 0, True)
    own_g_copy.wait()
    add_block(b, 0, s)
    for ds in range(1, ns):
        tb = lax.rem(s + ds, ns)
        g_landed(b, tb, 1 - c)
        add_block(b, 0, tb)

    for k in range(1, nb):
        if k > 1:
            relays(k, 0)
            a_relays(k + 1)
        if k > 1:
            from_left(k, lambda doc: doc_products(doc, 0, False))
            from_right(k, lambda doc: doc_products(doc, 1, False))
        for ds in range(1, ns):
            relays(k, ds)
        if k == 1:
            from_left(k, lambda doc: doc_products(doc, 0, False))
            from_right(k, lambda doc: doc_products(doc, 1, False))
        for ds in range(ns):
            add_blocks(k, ds)

    own_here = g_all.at[b, g_rows(s, c)]

    def take_products(side):
        y_z_copy(side, b).wait_recv()
        add_product(b, y_far.at[side], own_here)

    @pl.when(b == 1)
    def _():
        take_products(0)

    @pl.when(b == nb - 2)
    def _():
        take_products(1)

    mine[...] = jnp.concatenate([jnp.sum(part[j], axis=0, keepdims=True) for j in range(nb)], axis=0)

    def p_copy(t):
        return pltpu.make_async_remote_copy(
            src_ref=mine,
            dst_ref=others.at[t],
            send_sem=p_send.at[t],
            recv_sem=p_recv.at[t],
            device_id=device(*offsets(t)),
            device_id_type=MESH,
        )

    @pl.loop(1, n_dev)
    def _(t):
        p_copy(t).start()

    for ds in range(1, ns):
        x_copy(ds).wait_send()
        a_x_copy(a_panels.at[b], b, ds).wait_send()
    for db in range(1, nb):
        a_z_copy(db).wait_send()

    @pl.when(at_left_end)
    def _():
        y_side_copy.wait_send()
        y_z_copy(0, b + 1).wait_send()

    @pl.when(at_right_end)
    def _():
        y_side_copy.wait_send()
        y_z_copy(1, b - 1).wait_send()

    @pl.when(b < nb - 2)
    def _():
        right_copy(own_columns(s), b, s).wait_send()

    @pl.when(b > 1)
    def _():
        left_copy(own_columns(s), b, s).wait_send()

    for ds in range(1, ns):
        tb = lax.rem(s + ds, ns)
        src = g_all.at[b, g_rows(tb, c)]

        @pl.when((b < nb - 1) & (b > 0))
        def _():
            right_copy(src, b, tb).wait_send()
            left_copy(src, b, tb).wait_send()

        side_copy(b, tb).wait_send()

    def a_relay_sent(doc):
        for ds in range(1, ns):
            a_x_copy(a_all.at[doc, s], doc, ds).wait_send()

    def relay_sent(doc, tb, onward, may_go_on):
        @pl.when(may_go_on)
        def _():
            onward(g_all.at[doc, g_rows(tb, c)], doc, tb).wait_send()

        side_copy(doc, tb).wait_send()

    for k in range(1, nb):
        from_left(k, a_relay_sent)
        from_right(k, a_relay_sent)
        for ds in range(ns):
            tb = lax.rem(s + ds, ns)
            left, right = sides(k, ds)

            @pl.when(left)
            def _():
                relay_sent(b - k, tb, right_copy, b < nb - 1)

            @pl.when(right)
            def _():
                relay_sent(b + k, tb, left_copy, b > 0)

    @pl.loop(1, n_dev)
    def _(t):
        p_copy(t).wait()

    def add_one(t, total):
        return total + others[t]

    total = lax.fori_loop(1, n_dev, add_one, mine[...])
    chosen = jnp.zeros((1, 128), jnp.float32)
    for j in range(nb):
        chosen = chosen + jnp.where(assign_ref[j] == b, total[j:j + 1], 0.0)
    out_ref[...] = jnp.sum(chosen, axis=1, keepdims=True)


def on_device(activations, output_grads, queries, lengths, assignment):
    nb, ns, nc = lax.axis_size("blk"), lax.axis_size("seq"), lax.axis_size("col")
    rows = output_grads.shape[0]
    fp, dl = queries.shape[1], queries.shape[2]
    n_dev = nb * ns * nc
    dma = pltpu.SemaphoreType.DMA
    return pl.pallas_call(
        functools.partial(score_kernel, nb, ns, nc),
        out_shape=jax.ShapeDtypeStruct((1, 1), jnp.float32),
        in_specs=[
            pl.BlockSpec(memory_space=pl.ANY),
            pl.BlockSpec(memory_space=pl.ANY),
            pl.BlockSpec(memory_space=pl.ANY),
            pl.BlockSpec(memory_space=pltpu.SMEM),
            pl.BlockSpec(memory_space=pltpu.SMEM),
        ],
        out_specs=pl.BlockSpec(memory_space=pltpu.VMEM),
        scratch_shapes=[
            pltpu.VMEM((nb, ns * rows, dl), jnp.bfloat16),
            pltpu.VMEM((nb, ns, fp, rows), jnp.bfloat16),
            pltpu.VMEM((rows, nb * fp), jnp.bfloat16),
            pltpu.VMEM((nb, fp, rows), jnp.bfloat16),
            pltpu.VMEM((fp, dl), jnp.float32),
            pltpu.VMEM((fp, dl), jnp.bfloat16),
            pltpu.VMEM((fp, dl), jnp.bfloat16),
            pltpu.VMEM((ns * rows, fp), jnp.bfloat16),
            pltpu.VMEM((2, ns * rows, dl), jnp.float32),
            pltpu.VMEM((rows, dl), jnp.float32),
            pltpu.VMEM((rows // nc, dl), jnp.float32),
            pltpu.VMEM((rows // nc, dl), jnp.float32),
            pltpu.VMEM((2, rows // nc, dl), jnp.float32),
            pltpu.VMEM((nb, 8, 128), jnp.float32),
            pltpu.VMEM((nb, 128), jnp.float32),
            pltpu.VMEM((n_dev, nb, 128), jnp.float32),
            dma((3,)),
            dma((nb, ns, nc)),
            dma((nb, ns)),
            dma((nb, ns)),
            dma((nb, ns)),
            dma((max(ns - 1, 1),)),
            dma((nb, ns)),
            dma((max(nb - 1, 1),)),
            dma((nb, max(ns - 1, 1))),
            dma((2,)),
            dma((3,)),
            dma((n_dev,)),
            dma((n_dev,)),
        ],
        compiler_params=pltpu.CompilerParams(
            collective_id=0, has_side_effects=True, vmem_limit_bytes=56 * 1024 * 1024
        ),
        cost_estimate=pl.CostEstimate(
            flops=2 * nb * ns * rows * fp * dl, bytes_accessed=4 * fp * dl, transcendentals=0
        ),
    )(activations, output_grads, queries, lengths, assignment)


def solution(mesh):
    in_specs = (
        P(("grp", "blk", "seq"), "col"),
        P(("grp", "blk", "seq"), None),
        P("grp", ("col", "blk"), "seq"),
        P(("grp", "blk")),
        P("grp"),
    )
    out_specs = P(None, ("grp", "blk"))
    return jax.shard_map(
        on_device, mesh=mesh, in_specs=in_specs, out_specs=out_specs, check_vma=False
    )
```
